256 devices in a mesh: segment: 4 (over y), seq: 32 (over z, x_lo, core), tensor: 2 (over x_hi).
Axes of the slice: x: 4 (x_hi: 2, x_lo: 2; x = x_hi * 2 + x_lo), y: 4, z: 8, core: 2. Of those that a mesh axis runs over, the one named last changes fastest.
Arguments:
- self_q: bfloat16 [4, 4096, 32, 128], P('segment', 'seq', 'tensor'), may hold values from -24 to 24
- self_kv: bfloat16 [4, 4096, 4, 256], P('segment', 'seq', 'tensor'), may hold values from -4.5 to 4.5
- cross_q: bfloat16 [4, 4096, 32, 128], P('segment', 'seq', 'tensor'), may hold values from -24 to 24
- vision_kv: bfloat16 [1024, 4, 256], P(('segment', 'seq'), 'tensor'), may hold values from -4.5 to 4.5
- cross_gate: float32 [4, 32], P('segment', 'tensor'), may hold values from 0.3 to 1.5
- cross_mask: int32 [64, 4], P('seq'), may hold values 0 or 1
- image_tokens: int32 [4], replicated, may hold values from 1 to 512, 1024 in all
- out_cotangent: bfloat16 [4, 4096, 32, 128], P('segment', 'seq', 'tensor'), may hold values from -6 to 6
Outputs:
- mixed: bfloat16 [4, 4096, 32, 128], P('segment', 'seq', 'tensor')
- grad_cross_q: bfloat16 [4, 4096, 32, 128], P('segment', 'seq', 'tensor')
- grad_vision_kv: float32 [1024, 4, 256], P(('segment', 'seq'), 'tensor')
The draws below stay inside these ranges and needn't reach their ends.
Inputs may be any that keep to these rules, and one draw needn't show every extreme that they name: `image_tokens`: the counts sum to 1024.
All inputs are finite; a program needn't handle non-finite values. No bound on the sum of `cross_mask` on one device may be relied on, other than what follows from the above.
Results may differ from the reference program's by a relative error of at most 0.02.
Values may be sent and summed in bfloat16 or wider, within the bound.
No kernel may reach another device: no remote copies, remote signals or barrier semaphores. Data moves between devices by JAX's collectives and lax.ppermute only.
A program may use at most 64 MiB of HBM per device.

```python
import math
import jax
import jax.numpy as jnp
import numpy as np
from jax import lax

HD = 128
QH = 32
KVH = 4
IMAGES = 4
BLOCK = 64
SECT = 4
TOKENS = 4096
NV = 1024
TEXT_BLOCKS = 64


def blend_normal(key, shape):
    normal_key = jax.random.fold_in(key, 0)
    normal_part = jax.random.truncated_normal(normal_key, -4.0, 4.0, shape, jnp.float32)
    return normal_part


def text_key_rows(key):
    base_rows = blend_normal(jax.random.fold_in(key, 101), (SECT, TOKENS, KVH, HD))
    position = jnp.arange(TOKENS, dtype=jnp.int32)
    twin_rows = (position % 61 == 34)[None, :, None, None]
    tied_rows = base_rows
    return jnp.where(twin_rows, tied_rows, base_rows)


def vision_key_rows(key):
    base_rows = blend_normal(jax.random.fold_in(key, 202), (NV, KVH, HD))
    position = jnp.arange(NV, dtype=jnp.int32)
    twin_rows = (position % 29 == 6)[:, None, None]
    tied_rows = base_rows
    return jnp.where(twin_rows, tied_rows, base_rows)


def draw_self_kv(key, part):
    key_rows = text_key_rows(key)
    key = jax.random.fold_in(key, 3)
    value_rows = blend_normal(key, (SECT, TOKENS, KVH, HD))
    return jnp.concatenate([key_rows, value_rows], axis=-1).astype(jnp.bfloat16)


def draw_self_q(key, part):
    key = jax.random.fold_in(key, 5)
    base_rows = blend_normal(key, (SECT, TOKENS, QH, HD))
    position = jnp.arange(TOKENS, dtype=jnp.int32)
    chosen = (position % 61 == 37)[None, :, None, None]
    aligned = base_rows
    return jnp.where(chosen, aligned, base_rows).astype(jnp.bfloat16)


def draw_vision_kv(key, part):
    key_rows = vision_key_rows(key)
    key = jax.random.fold_in(key, 7)
    value_rows = blend_normal(key, (NV, KVH, HD))
    return jnp.concatenate([key_rows, value_rows], axis=-1).astype(jnp.bfloat16)


def draw_cross_q(key, part):
    key = jax.random.fold_in(key, 9)
    base_rows = blend_normal(key, (SECT, TOKENS, QH, HD))
    position = jnp.arange(TOKENS, dtype=jnp.int32)
    chosen = (position % 53 == 20)[None, :, None, None]
    aligned = base_rows
    return jnp.where(chosen, aligned, base_rows).astype(jnp.bfloat16)


def touch_ends(entries, stream_key, low, largest):
    place = [jax.random.randint(jax.random.fold_in(stream_key, axis), (), 0, length) for axis, length in enumerate(entries.shape)]
    widest = entries.shape.index(max(entries.shape))
    beside = place[:widest] + [(place[widest] + 1) % entries.shape[widest]] + place[widest + 1:]
    return entries.at[tuple(place)].set(low).at[tuple(beside)].set(largest)


def levels(rng, extent, cuts, least, largest):
    loudness, own = 1.0, jax.random.fold_in(rng, 6)
    for dim, blocks in cuts:
        steps = jnp.exp(jax.random.uniform(jax.random.fold_in(own, dim), (blocks,), jnp.float32, least / len(cuts), largest / len(cuts)))
        loudness = loudness * jnp.repeat(steps, extent[dim] // blocks).reshape([-1 if axis == dim else 1 for axis in range(len(extent))])
    return loudness


def length_profile(number_of, total, bound, skew):
    loads = [(1 << 20) // math.isqrt(standing ** skew) + 1 for standing in range(2, number_of + 1)]
    spare, holding = total - bound - (number_of - 1), [1] * (number_of - 1)
    while spare > 0:
        candidates = [i for i in range(number_of - 1) if holding[i] < bound]
        mass, remaining = sum([loads[i] for i in candidates]), spare
        for i in candidates:
            more = min(bound - holding[i], max(1, remaining * loads[i] // mass), spare)
            holding[i] = holding[i] + more
            spare = spare - more
    return np.array([bound] + holding)


def ragged(own_key, count, total, limit, slope):
    if count == 2:
        one = jax.random.randint(own_key, (), max(1, total - limit), min(limit, total - 1) + 1)
        return jnp.stack([one, total - one])
    sizes = jnp.asarray(length_profile(count, total, limit, slope), jnp.int32)
    couples = (count - 1) // 2
    giver, receiver = sizes[1:1 + 2 * couples:2], sizes[2:2 + 2 * couples:2]
    slack = jnp.minimum(giver - 1, limit - receiver)
    moved = jax.random.randint(jax.random.fold_in(own_key, 1), (couples,), 0, 1 << 20) % (slack + 1)
    sizes = sizes.at[1:1 + 2 * couples:2].set(giver - moved).at[2:2 + 2 * couples:2].set(receiver + moved)
    return sizes[jax.random.permutation(jax.random.fold_in(own_key, 2), count)]


def noise(key, dims, scale, reach, cuts=(), held_as=jnp.bfloat16):
    level = levels(key, dims, cuts, -0.22, 0.18) if cuts else 1.0
    result = jax.random.normal(key, dims, jnp.float32) * scale * level
    return jnp.minimum(jnp.maximum(result, -reach), reach).astype(held_as)


def setup_inputs(seed: int = 0) -> dict:
    splits = jax.random.split(jax.random.key(seed), 9)
    return {
        "self_q": draw_self_q(jax.random.fold_in(splits[8], 71), 0),
        "self_kv": draw_self_kv(jax.random.fold_in(splits[8], 71), 0),
        "cross_q": draw_cross_q(jax.random.fold_in(splits[8], 71), 0),
        "vision_kv": draw_vision_kv(jax.random.fold_in(splits[8], 71), 0),
        "cross_gate": jnp.clip(0.3 + 1.2 * jax.random.uniform(splits[4], (SECT, QH), jnp.float32) ** levels(splits[4], (SECT, QH), ((0, 4), (1, 2)), -0.2, 0.2), 0.3, 1.5),
        "cross_mask": touch_ends((jax.random.randint(splits[5], (TEXT_BLOCKS, IMAGES), 0, 3) < 2).astype(jnp.int32), jax.random.fold_in(splits[5], 1), 0, 1),
        "image_tokens": ragged(splits[6], IMAGES, NV, NV // 2, 2).astype(jnp.int32),
        "out_cotangent": noise(splits[7], (SECT, TOKENS, QH, HD), 1.0, 6.0, ((0, 4), (1, 32), (2, 2))),
    }


def round_keep(values):
    return lax.optimization_barrier(values.astype(jnp.bfloat16)).astype(jnp.float32)

def image_index(image_tokens, token_count):
    bounds = jnp.cumsum(image_tokens).astype(jnp.int32)
    column = jnp.arange(token_count, dtype=jnp.int32)
    return lax.optimization_barrier(jnp.sum((column[:, None] >= bounds[None, :-1]).astype(jnp.int32), axis=1))

def reference(self_q, self_kv, cross_q, vision_kv, cross_gate, cross_mask, image_tokens, out_cotangent):
    score_scale = 1.0 / math.sqrt(HD)
    groups = QH // KVH
    row_block = math.gcd(TOKENS, 512)
    block_count = TOKENS // row_block
    vision_keys = vision_kv[:, :, :HD].astype(jnp.float32)
    vision_values = vision_kv[:, :, HD:].astype(jnp.float32)
    image_of = image_index(image_tokens, NV)
    one_hot = (image_of[None, :] == jnp.arange(IMAGES, dtype=jnp.int32)[:, None]).astype(jnp.float32)
    text_mask = jnp.repeat(cross_mask, BLOCK, axis=0).astype(jnp.float32)
    live_all = jnp.dot(text_mask, one_hot, precision=lax.Precision.HIGHEST) > 0.5
    positions = jnp.arange(TOKENS, dtype=jnp.int32)
    grad_keys = jnp.zeros((NV, KVH, HD), jnp.float32)
    grad_values = jnp.zeros((NV, KVH, HD), jnp.float32)
    mixed_parts = []
    grad_parts = []
    for section in range(SECT):
        text_keys = self_kv[section, :, :, :HD].astype(jnp.float32)
        text_values = self_kv[section, :, :, HD:].astype(jnp.float32)
        gate_value = jnp.tanh(cross_gate[section]).reshape(KVH, groups)
        stacked = (jnp.arange(block_count, dtype=jnp.int32), self_q[section].reshape(block_count, row_block, KVH, groups, HD), cross_q[section].reshape(block_count, row_block, KVH, groups, HD), out_cotangent[section].reshape(block_count, row_block, KVH, groups, HD), live_all.reshape(block_count, row_block, NV))

        def one_block(sums_in, inputs):
            key_sum, value_sum = sums_in
            block_index, query_rows, cross_rows, cotangent_rows, live_rows = inputs
            row_ids = block_index * row_block + jnp.arange(row_block, dtype=jnp.int32)
            scores = jnp.einsum('rkgd,nkd->kgrn', query_rows.astype(jnp.float32), text_keys) * score_scale
            causal = positions[None, :] <= row_ids[:, None]
            row_max = lax.optimization_barrier(jnp.max(jnp.where(causal, scores, -1e+30), axis=-1))
            weights = jnp.where(causal, jnp.exp(scores - row_max[..., None]), 0.0)
            self_out = jnp.einsum('kgrn,nkd->kgrd', round_keep(weights), text_values) / lax.optimization_barrier(jnp.sum(weights, axis=-1))[..., None]
            cross_scores = jnp.einsum('rkgd,nkd->kgrn', cross_rows.astype(jnp.float32), vision_keys) * score_scale
            cross_max = lax.optimization_barrier(jnp.max(jnp.where(live_rows, cross_scores, -1e+30), axis=-1))
            cross_weights = jnp.where(live_rows, jnp.exp(cross_scores - cross_max[..., None]), 0.0)
            cross_total = jnp.maximum(lax.optimization_barrier(jnp.sum(cross_weights, axis=-1)), 1.0)
            cross_out = jnp.einsum('kgrn,nkd->kgrd', round_keep(cross_weights), vision_values) / cross_total[..., None]
            mixed_block = self_out + gate_value[:, :, None, None] * cross_out
            mixed_block = jnp.transpose(mixed_block, (2, 0, 1, 3)).reshape(row_block, QH, HD).astype(jnp.bfloat16)
            grad_out = round_keep(gate_value[None, :, :, None] * cotangent_rows.astype(jnp.float32))
            row_dot = lax.optimization_barrier(jnp.sum(jnp.transpose(grad_out, (1, 2, 0, 3)) * cross_out, axis=-1))
            cross_probs = cross_weights / cross_total[..., None]
            prob_grad = jnp.einsum('rkgd,nkd->kgrn', grad_out, vision_values)
            score_grad = round_keep(cross_probs * (prob_grad - row_dot[..., None]) * score_scale)
            query_grad = jnp.einsum('kgrn,nkd->rkgd', score_grad, vision_keys).reshape(row_block, QH, HD).astype(jnp.bfloat16)
            key_sum = key_sum + jnp.einsum('kgrn,rkgd->nkd', score_grad, cross_rows.astype(jnp.float32))
            value_sum = value_sum + jnp.einsum('kgrn,rkgd->nkd', round_keep(cross_probs), grad_out)
            return ((key_sum, value_sum), (mixed_block, query_grad))
        (grad_keys, grad_values), (mixed_stack, grad_stack) = lax.scan(one_block, (grad_keys, grad_values), stacked)
        mixed_parts.append(mixed_stack.reshape(TOKENS, QH, HD))
        grad_parts.append(grad_stack.reshape(TOKENS, QH, HD))
    return (jnp.stack(mixed_parts), jnp.stack(grad_parts), jnp.concatenate([grad_keys, grad_values], axis=-1))
```

```python
import math

import jax
import jax.numpy as jnp
from jax import lax
from jax.experimental import pallas as pl
from jax.experimental.pallas import tpu as pltpu
from jax.sharding import Mesh, PartitionSpec as P

IMAGES = 4
BLOCK = 64
HD = 128
NEG = -1e30
F32 = jnp.float32
BF16 = jnp.bfloat16
SCALE = 1.0 / math.sqrt(HD)
SCALE2 = SCALE / math.log(2.0)
NT = (((1,), (1,)), ((), ()))


def nt(a, b):
    return lax.dot_general(a, b, NT, preferred_element_type=F32)


def nn(a, b):
    return jnp.dot(a, b, preferred_element_type=F32)


def flip(a):
    return jnp.transpose(a.astype(F32), (1, 0)).astype(a.dtype)


def cross_kernel(
    info_ref,
    cq_ref,
    cot_ref,
    gate_col_ref,
    gate_row_ref,
    va_ref,
    vb_ref,
    out_ref,
    gq_ref,
    ga_ref,
    gb_ref,
    bias_ref,
):
    half = va_ref.shape[0]
    core = info_ref[11]
    pos = lax.broadcasted_iota(jnp.int32, (half, HD), 0)
    for side in range(2):
        which = core if side == 0 else 1 - core
        token = (2 * (pos // 8) + which) * 8 + pos % 8
        for rb in range(2):
            on = jnp.zeros((half, HD), jnp.int32) + info_ref[3 + rb * IMAGES]
            for k in range(IMAGES - 1):
                on = jnp.where(token >= info_ref[k], info_ref[3 + rb * IMAGES + k + 1], on)
            bias_ref[rb, pl.ds(side * half, half), :] = jnp.where(on == 1, 0.0, NEG)

    rows = BLOCK * 8
    for h in range(2):
        lane = h * 2 * HD
        ka, kb = va_ref[:, lane : lane + HD], vb_ref[:, lane : lane + HD]
        wa, wb = va_ref[:, lane + HD : lane + 2 * HD], vb_ref[:, lane + HD : lane + 2 * HD]
        keys = jnp.concatenate([ka, kb], axis=0)
        values = jnp.concatenate([wa, wb], axis=0)
        keys_t, values_t = flip(keys), flip(values)
        gk = None
        for rb in range(2):
            r0 = rb * BLOCK
            q = cq_ref[r0 : r0 + BLOCK, h * 8 : h * 8 + 8, :].reshape(rows, HD)
            cot = cot_ref[r0 : r0 + BLOCK, h * 8 : h * 8 + 8, :].astype(F32)
            go = (cot * gate_col_ref[h * 8 : h * 8 + 8, :][None]).astype(BF16).reshape(rows, HD)
            s = nt(keys, q) * SCALE2 + jnp.tile(bias_ref[rb], (1, rows // HD))
            top = jnp.max(s, axis=0, keepdims=True)
            top = jnp.where(top < 0.5 * NEG, 0.0, top)
            p = jnp.exp2(s - top)
            inv = 1.0 / jnp.maximum(jnp.sum(p, axis=0, keepdims=True), 1.0)
            pb = p.astype(BF16)
            cross = nn(values_t, pb) * inv
            out_ref[h, :, rb * rows : (rb + 1) * rows] = cross * gate_row_ref[h : h + 1, :]
            go_t = jnp.transpose(go.astype(F32), (1, 0))
            dot = jnp.sum(go_t * cross, axis=0, keepdims=True)
            ds = (p * (nt(values, go) - dot)).astype(BF16)
            dq = nn(keys_t, ds) * (inv * SCALE)
            gq_ref[r0 : r0 + BLOCK, h * 8 : h * 8 + 8, :] = (
                jnp.transpose(dq, (1, 0)).reshape(BLOCK, 8, HD).astype(BF16)
            )
            inv_col = jnp.transpose(jnp.broadcast_to(inv, (HD, rows)), (1, 0))
            qs = (q.astype(F32) * (inv_col * SCALE)).astype(BF16)
            gs = (go.astype(F32) * inv_col).astype(BF16)
            dk, dv = nn(ds, qs), nn(pb, gs)
            if rb == 0:
                gk, gv = dk, dv
            else:
                gk, gv = gk + dk, gv + dv
        ga_ref[:, lane : lane + HD] = gk[:half]
        ga_ref[:, lane + HD : lane + 2 * HD] = gv[:half]
        gb_ref[:, lane : lane + HD] = gk[half:].astype(BF16)
        gb_ref[:, lane + HD : lane + 2 * HD] = gv[half:].astype(BF16)


CHUNK = 512


def self_kernel(info_ref, q_ref, kva_ref, kvb_ref, cross_ref, out_ref, acc_ref, top_ref, sum_ref):
    own = info_ref[0]
    core = info_ref[1]
    rows = BLOCK * 8
    acc_ref[...] = jnp.zeros_like(acc_ref)
    top_ref[...] = jnp.full_like(top_ref, NEG)
    sum_ref[...] = jnp.zeros_like(sum_ref)

    def step(kv_ref, chunk, limits):
        start = pl.multiple_of(chunk * CHUNK, CHUNK)
        for h in range(2):
            lane = h * 2 * HD
            keys = kv_ref[pl.ds(start, CHUNK), lane : lane + HD]
            values_t = flip(kv_ref[pl.ds(start, CHUNK), lane + HD : lane + 2 * HD])
            for rb in range(2):
                r0 = rb * BLOCK
                cols = slice(rb * rows, (rb + 1) * rows)
                q = q_ref[r0 : r0 + BLOCK, h * 8 : h * 8 + 8, :].reshape(rows, HD)
                s = nt(keys, q) * SCALE2
                if limits is not None:
                    key = lax.broadcasted_iota(jnp.int32, (CHUNK, rows), 0)
                    s = jnp.where(key <= limits[rb] - start, s, NEG)
                old = top_ref[h : h + 1, cols]
                top = jnp.maximum(old, jnp.max(s, axis=0, keepdims=True))
                factor = jnp.exp2(old - top)
                p = jnp.exp2(s - top)
                sum_ref[h : h + 1, cols] = sum_ref[h : h + 1, cols] * factor + jnp.sum(
                    p, axis=0, keepdims=True
                )
                top_ref[h : h + 1, cols] = top
                acc_ref[h, :, cols] = acc_ref[h, :, cols] * factor + nn(values_t, p.astype(BF16))

    def side(kv_ref, full, limits, partial):
        @pl.loop(0, full)
        def _(chunk):
            step(kv_ref, chunk, None)

        @pl.when(partial)
        def _():
            step(kv_ref, full, limits)

    row = lax.broadcasted_iota(jnp.int32, (1, rows), 1) // 8
    per = CHUNK // 128
    side(kva_ref, own // per, [own * 128 + rb * BLOCK + row for rb in range(2)], own >= 0)
    count = own + core
    side(kvb_ref, count // per, [0 * row + count * 128 - 1] * 2, count % per > 0)
    for h in range(2):
        mixed = acc_ref[h] * (1.0 / sum_ref[h : h + 1, :]) + cross_ref[h]
        out_ref[:, h * 8 : h * 8 + 8, :] = (
            jnp.transpose(mixed, (1, 0)).reshape(2 * BLOCK, 8, HD).astype(BF16)
        )


def spec():
    return pl.BlockSpec(memory_space=pltpu.VMEM)


def shards(
    self_q, self_kv, cross_q, vision_kv, cross_gate, cross_mask, image_tokens, out_cotangent
):
    x = lax.axis_index("x")
    core = lax.axis_index("c")
    swap = [(0, 1), (1, 0)]
    ring = ("y", "z", "x")
    parts = lax.axis_size(ring)
    kv = self_kv.reshape(128, 4 * HD)
    other = lax.ppermute(kv, "x", swap)
    pair = jnp.where(x == 0, jnp.stack([kv, other]), jnp.stack([other, kv]))
    kva = lax.all_gather(pair.reshape(256, 4 * HD), "z", axis=0, tiled=True)
    kvb = lax.ppermute(kva, "c", swap)

    image = vision_kv.reshape(8, 4 * HD)
    tokens = parts * 8
    va = lax.all_to_all(
        jnp.broadcast_to(image[None], (parts, 8, 4 * HD)), ring, 0, 0, tiled=True
    ).reshape(tokens, 4 * HD)
    vb = lax.ppermute(va, "c", swap)

    gate = jnp.tanh(cross_gate[0])
    gate_col = jnp.broadcast_to(gate[:, None], (16, HD))
    gate_row = jnp.tile(gate.reshape(2, 8), (1, BLOCK))
    bounds = jnp.cumsum(image_tokens)[: IMAGES - 1]
    info = jnp.concatenate(
        [bounds, cross_mask.reshape(2 * IMAGES), jnp.stack([core, core])]
    ).astype(jnp.int32)

    smem = pl.BlockSpec(memory_space=pltpu.SMEM)
    cross_t, grad_q, grad_own, grad_other = pl.pallas_call(
        cross_kernel,
        out_shape=(
            jax.ShapeDtypeStruct((2, HD, 1024), F32),
            jax.ShapeDtypeStruct((128, 16, HD), BF16),
            jax.ShapeDtypeStruct((tokens, 4 * HD), F32),
            jax.ShapeDtypeStruct((tokens, 4 * HD), BF16),
        ),
        in_specs=[smem] + [spec()] * 6,
        out_specs=[spec()] * 4,
        scratch_shapes=[pltpu.VMEM((2, 2 * tokens, HD), F32)],
        compiler_params=pltpu.CompilerParams(vmem_limit_bytes=48 << 20),
        cost_estimate=pl.CostEstimate(
            flops=6 * 2 * 2 * 1024 * 1024 * 128, bytes_accessed=6 << 20, transcendentals=2 << 20
        ),
        name="cross_attention",
    )(info, cross_q[0], out_cotangent[0], gate_col, gate_row, va, vb)

    received = lax.ppermute(grad_other, "c", swap)
    partial = (grad_own + received.astype(F32)).astype(BF16).reshape(parts, 8, 4 * HD)
    pieces = lax.all_to_all(partial, ring, 0, 0, tiled=True)

    own = lax.axis_index("z") * 2 + x
    mixed = pl.pallas_call(
        self_kernel,
        out_shape=jax.ShapeDtypeStruct((128, 16, HD), BF16),
        in_specs=[smem] + [spec()] * 4,
        out_specs=spec(),
        scratch_shapes=[
            pltpu.VMEM((2, HD, 1024), F32),
            pltpu.VMEM((2, 1024), F32),
            pltpu.VMEM((2, 1024), F32),
        ],
        compiler_params=pltpu.CompilerParams(vmem_limit_bytes=48 << 20),
        cost_estimate=pl.CostEstimate(
            flops=2 * 2 * 2 * 4096 * 1024 * 128, bytes_accessed=6 << 20, transcendentals=8 << 20
        ),
        name="self_attention",
    )(jnp.stack([own, core]).astype(jnp.int32), self_q[0], kva, kvb, cross_t)

    image_grads = jnp.sum(pieces.astype(F32), axis=0).reshape(8, 2, 2 * HD)
    return (mixed[None], grad_q[None], image_grads)


def solution(mesh):
    fine = Mesh(mesh.devices.reshape(4, 8, 2, 2, 2), ("y", "z", "x", "c", "t"))
    rows = P("y", ("z", "x", "c"), "t", None)
    image = P(("y", "z", "x", "c"), "t", None)
    return jax.shard_map(
        shards,
        mesh=fine,
        in_specs=(rows, rows, rows, image, P("y", "t"), P(("z", "x", "c"), None), P(), rows),
        out_specs=(rows, rows, image),
        check_vma=False,
    )
```

```python
import math

import jax
import jax.numpy as jnp
from jax import lax
from jax.experimental import pallas as pl
from jax.experimental.pallas import tpu as pltpu
from jax.sharding import Mesh, PartitionSpec as P

IMAGES = 4
BLOCK = 64
HD = 128
NEG = -1e30
F32 = jnp.float32
BF16 = jnp.bfloat16
SCALE = 1.0 / math.sqrt(HD)
SCALE2 = SCALE / math.log(2.0)
NT = (((1,), (1,)), ((), ()))


def nt(a, b):
    return lax.dot_general(a, b, NT, preferred_element_type=F32)


def nn(a, b):
    return jnp.dot(a, b, preferred_element_type=F32)


def flip(a):
    return jnp.transpose(a.astype(F32), (1, 0)).astype(a.dtype)


def cross_kernel(
    image_ref,
    mask_ref,
    cq_ref,
    cot_ref,
    gate_ref,
    va_ref,
    vb_ref,
    out_ref,
    gq_ref,
    ga_ref,
    gb_ref,
):
    h = pl.program_id(0)
    core = lax.axis_index("c")
    half = va_ref.shape[0]
    count = 2 * half
    rows = cq_ref.shape[0] * 8
    lane = lax.broadcasted_iota(jnp.int32, (1, count), 1)
    which = jnp.where(lane < half, core, 1 - core)
    part = lane % half // 8
    token = (((part // 16 * 8 + part % 8) * 2 + part // 8 % 2) * 2 + which) * 8 + lane % 8
    live = []
    for rb in range(2):
        on = jnp.zeros((1, count), jnp.int32) + mask_ref[rb, 0]
        bound = 0
        for k in range(IMAGES - 1):
            bound = bound + image_ref[k]
            on = jnp.where(token >= bound, mask_ref[rb, k + 1], on)
        live.append(jnp.broadcast_to(jnp.where(on == 1, 0.0, NEG), (rows // 2, count)))
    bias = jnp.concatenate(live, axis=0)

    keys = jnp.concatenate([va_ref[:, :HD], vb_ref[:, :HD]], axis=0)
    values = jnp.concatenate([va_ref[:, HD:], vb_ref[:, HD:]], axis=0)
    head = lax.broadcasted_iota(jnp.int32, (8, 16), 0) + h * 8
    chosen = lax.broadcasted_iota(jnp.int32, (8, 16), 1) == head
    gates = jnp.where(chosen, jnp.broadcast_to(gate_ref[...], (8, 16)), 0.0)
    gate = jnp.tanh(jnp.broadcast_to(jnp.sum(gates, axis=1, keepdims=True), (8, HD)))

    q = cq_ref[...].reshape(rows, HD)
    go = (cot_ref[...].astype(F32) * gate[None]).astype(BF16).reshape(rows, HD)
    s = nt(q, keys) * SCALE2 + bias
    top = jnp.max(s, axis=1, keepdims=True)
    top = jnp.where(top < 0.5 * NEG, 0.0, top)
    p = jnp.exp2(s - top)
    pb = p.astype(BF16)
    both = nn(pb, with_ones(values))
    inv = 1.0 / jnp.maximum(both[:, HD:], 1.0)
    cross = both[:, :HD] * inv
    out_ref[...] = cross.reshape(rows // 8, 8, HD) * gate[None]
    dot = jnp.sum(go.astype(F32) * cross, axis=1, keepdims=True)
    ds = (p * (nt(go, values) - dot)).astype(BF16)
    gq_ref[...] = (nn(ds, keys) * (inv * SCALE)).reshape(rows // 8, 8, HD).astype(BF16)
    qs = (q.astype(F32) * (inv * SCALE)).astype(BF16)
    gs = (go.astype(F32) * inv).astype(BF16)
    dk = jnp.transpose(nn(flip(qs), ds), (1, 0))
    dv = jnp.transpose(nn(flip(gs), pb), (1, 0))
    ga_ref[:, :HD] = dk[:half]
    ga_ref[:, HD:] = dv[:half]
    gb_ref[:, :HD] = dk[half:].astype(BF16)
    gb_ref[:, HD:] = dv[half:].astype(BF16)


LOCAL = 512
TILE = 256


def attend(q, keys, values, limit, top, total, acc):
    s = nt(q, keys) * SCALE2
    if limit is not None:
        s = jnp.where(limit, s, NEG)
    new = jnp.maximum(top, jnp.broadcast_to(jnp.max(s, axis=1, keepdims=True), top.shape))
    factor = jnp.exp2(top - new)
    p = jnp.exp2(s - jnp.tile(new, (1, keys.shape[0] // HD))).astype(BF16)
    both = nn(p, values)
    return new, total * factor + both[:, HD:], acc * factor + both[:, :HD]


def with_ones(values):
    return jnp.concatenate([values, jnp.ones_like(values)], axis=1)


def fetch_blocks(own_refs, other_refs, kv_ref, sems):
    half = LOCAL // 2
    for i, pair in enumerate(zip(own_refs, other_refs)):
        for side, source in enumerate(pair):
            target = kv_ref.at[i, pl.ds(side * half, half), :]
            pltpu.make_async_copy(source, target, sems.at[i, side]).start()


def wait_block(kv_ref, sems, block):
    half = LOCAL // 2
    for side in range(2):
        place = kv_ref.at[block, pl.ds(side * half, half), :]
        pltpu.make_async_copy(place, place, sems.at[block, side]).wait()


def blend(q_own, kv_ref, block, top_ref, sum_ref, acc_ref):
    for h in range(2):
        lane = h * 2 * HD
        keys = kv_ref[block, :, lane : lane + HD]
        values = with_ones(kv_ref[block, :, lane + HD : lane + 2 * HD])
        for t in range(1024 // TILE):
            cols = slice(t * TILE, (t + 1) * TILE)
            state = top_ref[h, cols, :], sum_ref[h, cols, :], acc_ref[h, cols, :]
            state = attend(q_own[h, cols, :], keys, values, None, *state)
            top_ref[h, cols, :], sum_ref[h, cols, :], acc_ref[h, cols, :] = state


NEAR = 7
FAR = 1


def near_kernel(*refs):
    own_refs, other_refs = refs[:NEAR], refs[NEAR : 2 * NEAR]
    q_ref, acc_out, lse_out, kv_ref, acc_ref, top_ref, sum_ref, q_own, sems = refs[2 * NEAR :]
    fetch_blocks(own_refs, other_refs, kv_ref, sems)
    for h in range(2):
        q_own[h] = q_ref[:, h * 8 : h * 8 + 8, :].reshape(1024, HD)
    z = lax.axis_index("z")
    core = lax.axis_index("c")
    half = LOCAL // 2
    key = lax.broadcasted_iota(jnp.int32, (TILE, LOCAL), 1)
    from_core = jnp.where(key < half, core, 1 - core)
    place = key % half
    place = (place // 128) * 256 + from_core * 128 + place % 128
    row = lax.broadcasted_iota(jnp.int32, (TILE, LOCAL), 0) // 8
    row = row + lax.axis_index("x") * 256 + core * 128
    start = jnp.full((TILE, HD), NEG, F32)
    zero = jnp.zeros((TILE, HD), F32)
    wait_block(kv_ref, sems, 0)
    for h in range(2):
        lane = h * 2 * HD
        keys = kv_ref[0, :, lane : lane + HD]
        values = with_ones(kv_ref[0, :, lane + HD : lane + 2 * HD])
        for t in range(1024 // TILE):
            cols = slice(t * TILE, (t + 1) * TILE)
            limit = place <= row + t * (TILE // 8)
            state = attend(q_own[h, cols, :], keys, values, limit, start, zero, zero)
            top_ref[h, cols, :], sum_ref[h, cols, :], acc_ref[h, cols, :] = state

    @pl.loop(1, NEAR)
    def _(block):
        wait_block(kv_ref, sems, block)
        step = (block + 1) // 2

        @pl.when(jnp.where(block % 2 == 1, z >= step, z + step >= 8))
        def _():
            blend(q_own, kv_ref, block, top_ref, sum_ref, acc_ref)

    acc_out[...] = acc_ref[...] / sum_ref[...]
    lse_out[...] = top_ref[...] + jnp.log2(sum_ref[...])


def far_kernel(*refs):
    own_ref, other_ref, q_ref, acc_in, lse_in, cross_ref, out_ref = refs[:7]
    kv_ref, acc_ref, top_ref, sum_ref, q_own, sems = refs[7:]
    fetch_blocks([own_ref], [other_ref], kv_ref, sems)
    for h in range(2):
        q_own[h] = q_ref[:, h * 8 : h * 8 + 8, :].reshape(1024, HD)
    acc_ref[...] = acc_in[...]
    top_ref[...] = lse_in[...]
    sum_ref[...] = jnp.ones_like(sum_ref)
    wait_block(kv_ref, sems, 0)

    @pl.when(lax.axis_index("z") >= 4)
    def _():
        blend(q_own, kv_ref, 0, top_ref, sum_ref, acc_ref)

    for h in range(2):
        mixed = (acc_ref[h] / sum_ref[h]).reshape(2 * BLOCK, 8, HD)
        out_ref[:, h * 8 : h * 8 + 8, :] = (mixed + cross_ref[:, h * 8 : h * 8 + 8, :]).astype(BF16)


def sum_kernel(pieces_ref, out_ref):
    total = jnp.sum(pieces_ref[...].astype(F32), axis=0)
    for h in range(2):
        out_ref[:, h, :] = total[:, h * 2 * HD : (h + 1) * 2 * HD]


def pair_kernel(own_ref, other_ref, out_ref):
    x = lax.axis_index("x")
    rows = own_ref.shape[0]
    out_ref[pl.ds(pl.multiple_of(x * rows, rows), rows), :] = own_ref[...]
    out_ref[pl.ds(pl.multiple_of((1 - x) * rows, rows), rows), :] = other_ref[...]


def pick_kernel(first_ref, second_ref, out_ref):
    core = lax.axis_index("c")

    @pl.when(core == 0)
    def _():
        out_ref[...] = first_ref[...]

    @pl.when(core == 1)
    def _():
        out_ref[...] = second_ref[...]


def spec():
    return pl.BlockSpec(memory_space=pltpu.VMEM)


def shards(
    self_q, self_kv, cross_q, vision_kv, cross_gate, cross_mask, image_tokens, out_cotangent
):
    swap = [(0, 1), (1, 0)]
    up = [(i, (i + 1) % 8) for i in range(8)]
    down = [(i, (i + 7) % 8) for i in range(8)]
    ring = ("y", "x", "z")
    parts = lax.axis_size(ring)
    tokens = parts * 8
    tie = lax.optimization_barrier

    image = jnp.broadcast_to(vision_kv.reshape(1, 8, 4 * HD), (8, 8, 4 * HD))
    kv = self_kv.reshape(128, 4 * HD)
    other = lax.ppermute(kv, "x", swap)
    column = lax.all_to_all(image, "z", 0, 0, tiled=True).reshape(1, 64, 4 * HD)
    column, kv, other = tie((column, kv, other))
    pair = pl.pallas_call(
        pair_kernel,
        out_shape=jax.ShapeDtypeStruct((256, 4 * HD), BF16),
        in_specs=[spec()] * 2,
        out_specs=spec(),
        compiler_params=pltpu.CompilerParams(vmem_limit_bytes=4 << 20),
        name="pair",
    )(kv, other)
    va = lax.all_to_all(
        jnp.broadcast_to(column, (8, 64, 4 * HD)), ("y", "x"), 0, 0, tiled=True
    ).reshape(tokens, 4 * HD)
    up1, down1 = lax.ppermute(pair, "z", up), lax.ppermute(pair, "z", down)
    pair_c = lax.ppermute(pair, "c", swap)

    va, up1, down1, pair_c = tie((va, up1, down1, pair_c))
    vb = lax.ppermute(va, "c", swap)
    up2, down2 = lax.ppermute(up1, "z", up), lax.ppermute(down1, "z", down)
    up1c, down1c = lax.ppermute(up1, "c", swap), lax.ppermute(down1, "c", swap)

    smem = pl.BlockSpec(memory_space=pltpu.SMEM)
    by_head = pl.BlockSpec((128, 8, HD), lambda h: (0, h, 0))
    by_lane = pl.BlockSpec((tokens, 2 * HD), lambda h: (0, h))
    cross, grad_q, grad_own, grad_other = pl.pallas_call(
        cross_kernel,
        grid=(2,),
        out_shape=(
            jax.ShapeDtypeStruct((128, 16, HD), F32),
            jax.ShapeDtypeStruct((128, 16, HD), BF16),
            jax.ShapeDtypeStruct((tokens, 4 * HD), F32),
            jax.ShapeDtypeStruct((tokens, 4 * HD), BF16),
        ),
        in_specs=[smem, smem, by_head, by_head, spec(), by_lane, by_lane],
        out_specs=[by_head, by_head, by_lane, by_lane],
        compiler_params=pltpu.CompilerParams(vmem_limit_bytes=40 << 20),
        cost_estimate=pl.CostEstimate(
            flops=6 * 2 * 2 * 1024 * 1024 * 128, bytes_accessed=6 << 20, transcendentals=2 << 20
        ),
        name="cross_attention",
    )(image_tokens, cross_mask, cross_q[0], out_cotangent[0], cross_gate, va, vb)

    grad_other, up1c, down1c, up2, down2 = tie((grad_other, up1c, down1c, up2, down2))
    received = lax.ppermute(grad_other, "c", swap)
    up3, down3 = lax.ppermute(up2, "z", up), lax.ppermute(down2, "z", down)
    up2c, down2c = lax.ppermute(up2, "c", swap), lax.ppermute(down2, "c", swap)
    partial = (grad_own + received.astype(F32)).astype(BF16).reshape(parts, 8, 4 * HD)
    partial, up2c, down2c = tie((partial, up2c, down2c))
    pieces = lax.all_to_all(partial, ring, 0, 0, tiled=True)

    hbm = pl.BlockSpec(memory_space=pl.ANY)

    def scratch(count):
        return [
            pltpu.VMEM((count, LOCAL, 4 * HD), BF16),
            pltpu.VMEM((2, 1024, HD), F32),
            pltpu.VMEM((2, 1024, HD), F32),
            pltpu.VMEM((2, 1024, HD), F32),
            pltpu.VMEM((2, 1024, HD), BF16),
            pltpu.SemaphoreType.DMA((count, 2)),
        ]

    def cost(count):
        return pl.CostEstimate(
            flops=count * 2 * 2 * 2 * 512 * 1024 * 128,
            bytes_accessed=6 << 20,
            transcendentals=count << 20,
        )

    split = pl.pallas_call(
        pick_kernel,
        out_shape=jax.ShapeDtypeStruct(up3.shape, BF16),
        in_specs=[spec()] * 2,
        out_specs=spec(),
        compiler_params=pltpu.CompilerParams(vmem_limit_bytes=4 << 20),
        name="pick",
    )(up3, down3)
    halves = [
        (zi * 2 + ci, (zi + (1 if ci == 0 else 7)) % 8 * 2 + ci)
        for zi in range(8)
        for ci in range(2)
    ]
    last = lax.ppermute(split, ("z", "c"), halves)
    up3c, down3c = lax.ppermute(up3, "c", swap), lax.ppermute(down3, "c", swap)
    near = [pair, up1, down1, up2, down2, up3, down3]
    near += [pair_c, up1c, down1c, up2c, down2c, up3c, down3c]
    acc, lse = pl.pallas_call(
        near_kernel,
        out_shape=(jax.ShapeDtypeStruct((2, 1024, HD), F32),) * 2,
        in_specs=[hbm] * (2 * NEAR) + [spec()],
        out_specs=[spec()] * 2,
        scratch_shapes=scratch(NEAR),
        compiler_params=pltpu.CompilerParams(vmem_limit_bytes=24 << 20),
        cost_estimate=cost(NEAR),
        name="self_near",
    )(*near, self_q[0])

    last, acc = tie((last, acc))
    last_c = lax.ppermute(last, "c", swap)
    mixed = pl.pallas_call(
        far_kernel,
        out_shape=jax.ShapeDtypeStruct((128, 16, HD), BF16),
        in_specs=[hbm] * (2 * FAR) + [spec()] * 4,
        out_specs=spec(),
        scratch_shapes=scratch(FAR),
        compiler_params=pltpu.CompilerParams(vmem_limit_bytes=24 << 20),
        cost_estimate=cost(FAR),
        name="self_far",
    )(last, last_c, self_q[0], acc, lse, cross)

    pieces, mixed = tie((pieces, mixed))
    image_grads = pl.pallas_call(
        sum_kernel,
        out_shape=jax.ShapeDtypeStruct((8, 2, 2 * HD), F32),
        in_specs=[spec()],
        out_specs=spec(),
        name="sum_pieces",
    )(pieces)
    return (mixed[None], grad_q[None], image_grads)


def solution(mesh):
    fine = Mesh(mesh.devices.reshape(4, 8, 2, 2, 2), ("y", "z", "x", "c", "t"))
    rows = P("y", ("z", "x", "c"), "t", None)
    image = P(("y", "z", "x", "c"), "t", None)
    return jax.shard_map(
        shards,
        mesh=fine,
        in_specs=(rows, rows, rows, image, P("y", "t"), P(("z", "x", "c"), None), P(), rows),
        out_specs=(rows, rows, image),
        check_vma=False,
    )
```

```python
import math

import jax
import jax.numpy as jnp
from jax import lax
from jax.experimental import pallas as pl
from jax.experimental.pallas import tpu as pltpu
from jax.sharding import Mesh, PartitionSpec as P

IMAGES = 4
BLOCK = 64
HD = 128
NEG = -1e30
F32 = jnp.float32
BF16 = jnp.bfloat16
SCALE = 1.0 / math.sqrt(HD)
SCALE2 = SCALE / math.log(2.0)
NT = (((1,), (1,)), ((), ()))


def nt(a, b):
    return lax.dot_general(a, b, NT, preferred_element_type=F32)


def nn(a, b):
    return jnp.dot(a, b, preferred_element_type=F32)


def flip(a):
    return jnp.transpose(a.astype(F32), (1, 0)).astype(a.dtype)


def info_kernel(image_ref, mask_ref, gate_ref, bias_ref, gate_out):
    core = lax.axis_index("c")
    count = bias_ref.shape[1]
    half = count // 2
    lane = lax.broadcasted_iota(jnp.int32, (1, count), 1)
    which = jnp.where(lane < half, core, 1 - core)
    part = lane % half // 8
    token = (((part // 16 * 8 + part % 8) * 2 + part // 8 % 2) * 2 + which) * 8 + lane % 8
    for rb in range(2):
        on = jnp.zeros((1, count), jnp.int32) + mask_ref[rb, 0]
        bound = 0
        for k in range(IMAGES - 1):
            bound = bound + image_ref[k]
            on = jnp.where(token >= bound, mask_ref[rb, k + 1], on)
        bias_ref[rb : rb + 1, :] = jnp.where(on == 1, 0.0, NEG)
    head = lax.broadcasted_iota(jnp.int32, (16, 16), 0)
    chosen = lax.broadcasted_iota(jnp.int32, (16, 16), 1) == head
    gates = jnp.where(chosen, jnp.broadcast_to(gate_ref[...], (16, 16)), 0.0)
    gate_out[...] = jnp.tanh(jnp.broadcast_to(jnp.sum(gates, axis=1, keepdims=True), (16, HD)))


def cross_kernel(
    bias_ref, cq_ref, cot_ref, gate_ref, va_ref, vb_ref, out_ref, gq_ref, ga_ref, gb_ref
):
    half = va_ref.shape[0]
    count = 2 * half
    rows = cq_ref.shape[0] * 8
    bias = jnp.concatenate(
        [jnp.broadcast_to(bias_ref[rb : rb + 1, :], (rows // 2, count)) for rb in range(2)], axis=0
    )
    gate = gate_ref[...]
    keys = jnp.concatenate([va_ref[:, :HD], vb_ref[:, :HD]], axis=0)
    values = jnp.concatenate([va_ref[:, HD:], vb_ref[:, HD:]], axis=0)
    q = cq_ref[...].reshape(rows, HD)
    go = (cot_ref[...].astype(F32) * gate[None]).astype(BF16).reshape(rows, HD)
    s = nt(q, keys) * SCALE2 + bias
    top = jnp.max(s, axis=1, keepdims=True)
    top = jnp.where(top < 0.5 * NEG, 0.0, top)
    p = jnp.exp2(s - top)
    pb = p.astype(BF16)
    both = nn(pb, with_ones(values))
    inv = 1.0 / jnp.maximum(both[:, HD:], 1.0)
    cross = both[:, :HD] * inv
    out_ref[...] = cross.reshape(rows // 8, 8, HD) * gate[None]
    dot = jnp.sum(go.astype(F32) * cross, axis=1, keepdims=True)
    ds = (p * (nt(go, values) - dot)).astype(BF16)
    gq_ref[...] = (nn(ds, keys) * (inv * SCALE)).reshape(rows // 8, 8, HD).astype(BF16)
    qs = (q.astype(F32) * (inv * SCALE)).astype(BF16)
    gs = (go.astype(F32) * inv).astype(BF16)
    dk = jnp.transpose(nn(flip(qs), ds), (1, 0))
    dv = jnp.transpose(nn(flip(gs), pb), (1, 0))
    ga_ref[:, :HD] = dk[:half]
    ga_ref[:, HD:] = dv[:half]
    gb_ref[:, :HD] = dk[half:].astype(BF16)
    gb_ref[:, HD:] = dv[half:].astype(BF16)


LOCAL = 512
TILE = 256


def attend(q, keys, values, limit, top, total, acc):
    s = nt(q, keys) * SCALE2
    if limit is not None:
        s = jnp.where(limit, s, NEG)
    new = jnp.maximum(top, jnp.broadcast_to(jnp.max(s, axis=1, keepdims=True), top.shape))
    factor = jnp.exp2(top - new)
    p = jnp.exp2(s - jnp.tile(new, (1, keys.shape[0] // HD))).astype(BF16)
    both = nn(p, values)
    return new, total * factor + both[:, HD:], acc * factor + both[:, :HD]


def with_ones(values):
    return jnp.concatenate([values, jnp.ones_like(values)], axis=1)


def fetch_blocks(own_refs, other_refs, kv_ref, sems):
    half = LOCAL // 2
    for i, pair in enumerate(zip(own_refs, other_refs)):
        for side, source in enumerate(pair):
            target = kv_ref.at[i, pl.ds(side * half, half), :]
            pltpu.make_async_copy(source, target, sems.at[i, side]).start()


def wait_block(kv_ref, sems, block):
    half = LOCAL // 2
    for side in range(2):
        place = kv_ref.at[block, pl.ds(side * half, half), :]
        pltpu.make_async_copy(place, place, sems.at[block, side]).wait()


def blend(q_own, kv_ref, block, top_ref, sum_ref, acc_ref):
    for h in range(2):
        lane = h * 2 * HD
        keys = kv_ref[block, :, lane : lane + HD]
        values = with_ones(kv_ref[block, :, lane + HD : lane + 2 * HD])
        for t in range(1024 // TILE):
            cols = slice(t * TILE, (t + 1) * TILE)
            state = top_ref[h, cols, :], sum_ref[h, cols, :], acc_ref[h, cols, :]
            state = attend(q_own[h, cols, :], keys, values, None, *state)
            top_ref[h, cols, :], sum_ref[h, cols, :], acc_ref[h, cols, :] = state


NEAR = 7
FAR = 1


def near_kernel(*refs):
    own_refs, other_refs = refs[:NEAR], refs[NEAR : 2 * NEAR]
    q_ref, acc_out, lse_out, kv_ref, acc_ref, top_ref, sum_ref, q_own, sems = refs[2 * NEAR :]
    fetch_blocks(own_refs, other_refs, kv_ref, sems)
    for h in range(2):
        q_own[h] = q_ref[:, h * 8 : h * 8 + 8, :].reshape(1024, HD)
    z = lax.axis_index("z")
    core = lax.axis_index("c")
    half = LOCAL // 2
    key = lax.broadcasted_iota(jnp.int32, (TILE, LOCAL), 1)
    from_core = jnp.where(key < half, core, 1 - core)
    place = key % half
    place = (place // 128) * 256 + from_core * 128 + place % 128
    row = lax.broadcasted_iota(jnp.int32, (TILE, LOCAL), 0) // 8
    row = row + lax.axis_index("x") * 256 + core * 128
    start = jnp.full((TILE, HD), NEG, F32)
    zero = jnp.zeros((TILE, HD), F32)
    wait_block(kv_ref, sems, 0)
    for h in range(2):
        lane = h * 2 * HD
        keys = kv_ref[0, :, lane : lane + HD]
        values = with_ones(kv_ref[0, :, lane + HD : lane + 2 * HD])
        for t in range(1024 // TILE):
            cols = slice(t * TILE, (t + 1) * TILE)
            limit = place <= row + t * (TILE // 8)
            state = attend(q_own[h, cols, :], keys, values, limit, start, zero, zero)
            top_ref[h, cols, :], sum_ref[h, cols, :], acc_ref[h, cols, :] = state

    @pl.loop(1, NEAR)
    def _(block):
        wait_block(kv_ref, sems, block)
        step = (block + 1) // 2

        @pl.when(jnp.where(block % 2 == 1, z >= step, z + step >= 8))
        def _():
            blend(q_own, kv_ref, block, top_ref, sum_ref, acc_ref)

    acc_out[...] = acc_ref[...] / sum_ref[...]
    lse_out[...] = top_ref[...] + jnp.log2(sum_ref[...])


def far_kernel(*refs):
    own_ref, other_ref, q_ref, acc_in, lse_in, cross_ref, out_ref = refs[:7]
    kv_ref, acc_ref, top_ref, sum_ref, q_own, sems = refs[7:]
    fetch_blocks([own_ref], [other_ref], kv_ref, sems)
    for h in range(2):
        q_own[h] = q_ref[:, h * 8 : h * 8 + 8, :].reshape(1024, HD)
    acc_ref[...] = acc_in[...]
    top_ref[...] = lse_in[...]
    sum_ref[...] = jnp.ones_like(sum_ref)
    wait_block(kv_ref, sems, 0)

    @pl.when(lax.axis_index("z") >= 4)
    def _():
        blend(q_own, kv_ref, 0, top_ref, sum_ref, acc_ref)

    for h in range(2):
        mixed = (acc_ref[h] / sum_ref[h]).reshape(2 * BLOCK, 8, HD)
        out_ref[:, h * 8 : h * 8 + 8, :] = (mixed + cross_ref[:, h * 8 : h * 8 + 8, :]).astype(BF16)


def sum_kernel(pieces_ref, out_ref):
    total = jnp.sum(pieces_ref[...].astype(F32), axis=0)
    for h in range(2):
        out_ref[:, h, :] = total[:, h * 2 * HD : (h + 1) * 2 * HD]


def pair_kernel(own_ref, other_ref, out_ref):
    x = lax.axis_index("x")
    rows = own_ref.shape[0]
    out_ref[pl.ds(pl.multiple_of(x * rows, rows), rows), :] = own_ref[...]
    out_ref[pl.ds(pl.multiple_of((1 - x) * rows, rows), rows), :] = other_ref[...]


def pick_kernel(first_ref, second_ref, out_ref):
    core = lax.axis_index("c")

    @pl.when(core == 0)
    def _():
        out_ref[...] = first_ref[...]

    @pl.when(core == 1)
    def _():
        out_ref[...] = second_ref[...]


def spec():
    return pl.BlockSpec(memory_space=pltpu.VMEM)


def shards(
    self_q, self_kv, cross_q, vision_kv, cross_gate, cross_mask, image_tokens, out_cotangent
):
    swap = [(0, 1), (1, 0)]
    up = [(i, (i + 1) % 8) for i in range(8)]
    down = [(i, (i + 7) % 8) for i in range(8)]
    ring = ("y", "x", "z")
    parts = lax.axis_size(ring)
    tokens = parts * 8
    tie = lax.optimization_barrier

    image = jnp.broadcast_to(vision_kv.reshape(1, 8, 4 * HD), (8, 8, 4 * HD))
    kv = self_kv.reshape(128, 4 * HD)
    other = lax.ppermute(kv, "x", swap)
    column = lax.all_to_all(image, "z", 0, 0, tiled=True).reshape(1, 64, 4 * HD)
    column, kv, other = tie((column, kv, other))
    pair = pl.pallas_call(
        pair_kernel,
        out_shape=jax.ShapeDtypeStruct((256, 4 * HD), BF16),
        in_specs=[spec()] * 2,
        out_specs=spec(),
        compiler_params=pltpu.CompilerParams(vmem_limit_bytes=4 << 20),
        name="pair",
    )(kv, other)
    va = lax.all_to_all(
        jnp.broadcast_to(column, (8, 64, 4 * HD)), ("y", "x"), 0, 0, tiled=True
    ).reshape(tokens, 4 * HD)
    up1, down1 = lax.ppermute(pair, "z", up), lax.ppermute(pair, "z", down)
    pair_c = lax.ppermute(pair, "c", swap)

    smem = pl.BlockSpec(memory_space=pltpu.SMEM)
    bias, gate = pl.pallas_call(
        info_kernel,
        out_shape=(
            jax.ShapeDtypeStruct((2, 2 * tokens), F32),
            jax.ShapeDtypeStruct((16, HD), F32),
        ),
        in_specs=[smem, smem, spec()],
        out_specs=[spec()] * 2,
        compiler_params=pltpu.CompilerParams(vmem_limit_bytes=4 << 20),
        name="mask_and_gate",
    )(image_tokens, cross_mask, cross_gate)
    va, up1, down1, pair_c, bias, gate = tie((va, up1, down1, pair_c, bias, gate))
    vb = lax.ppermute(va, "c", swap)
    up2, down2 = lax.ppermute(up1, "z", up), lax.ppermute(down1, "z", down)
    up1c, down1c = lax.ppermute(up1, "c", swap), lax.ppermute(down1, "c", swap)

    by_head = pl.BlockSpec((128, 8, HD), lambda h: (0, h, 0))
    by_lane = pl.BlockSpec((tokens, 2 * HD), lambda h: (0, h))
    cross, grad_q, grad_own, grad_other = pl.pallas_call(
        cross_kernel,
        grid=(2,),
        out_shape=(
            jax.ShapeDtypeStruct((128, 16, HD), F32),
            jax.ShapeDtypeStruct((128, 16, HD), BF16),
            jax.ShapeDtypeStruct((tokens, 4 * HD), F32),
            jax.ShapeDtypeStruct((tokens, 4 * HD), BF16),
        ),
        in_specs=[
            spec(),
            by_head,
            by_head,
            pl.BlockSpec((8, HD), lambda h: (h, 0)),
            by_lane,
            by_lane,
        ],
        out_specs=[by_head, by_head, by_lane, by_lane],
        compiler_params=pltpu.CompilerParams(vmem_limit_bytes=40 << 20),
        cost_estimate=pl.CostEstimate(
            flops=6 * 2 * 2 * 1024 * 1024 * 128, bytes_accessed=6 << 20, transcendentals=2 << 20
        ),
        name="cross_attention",
    )(bias, cross_q[0], out_cotangent[0], gate, va, vb)

    grad_other, up1c, down1c, up2, down2 = tie((grad_other, up1c, down1c, up2, down2))
    received = lax.ppermute(grad_other, "c", swap)
    up3, down3 = lax.ppermute(up2, "z", up), lax.ppermute(down2, "z", down)
    up2c, down2c = lax.ppermute(up2, "c", swap), lax.ppermute(down2, "c", swap)
    partial = (grad_own + received.astype(F32)).astype(BF16).reshape(parts, 8, 4 * HD)
    partial, up2c, down2c = tie((partial, up2c, down2c))
    pieces = lax.all_to_all(partial, ring, 0, 0, tiled=True)

    hbm = pl.BlockSpec(memory_space=pl.ANY)

    def scratch(count):
        return [
            pltpu.VMEM((count, LOCAL, 4 * HD), BF16),
            pltpu.VMEM((2, 1024, HD), F32),
            pltpu.VMEM((2, 1024, HD), F32),
            pltpu.VMEM((2, 1024, HD), F32),
            pltpu.VMEM((2, 1024, HD), BF16),
            pltpu.SemaphoreType.DMA((count, 2)),
        ]

    def cost(count):
        return pl.CostEstimate(
            flops=count * 2 * 2 * 2 * 512 * 1024 * 128,
            bytes_accessed=6 << 20,
            transcendentals=count << 20,
        )

    split = pl.pallas_call(
        pick_kernel,
        out_shape=jax.ShapeDtypeStruct(up3.shape, BF16),
        in_specs=[spec()] * 2,
        out_specs=spec(),
        compiler_params=pltpu.CompilerParams(vmem_limit_bytes=4 << 20),
        name="pick",
    )(up3, down3)
    halves = [
        (zi * 2 + ci, (zi + (1 if ci == 0 else 7)) % 8 * 2 + ci)
        for zi in range(8)
        for ci in range(2)
    ]
    last = lax.ppermute(split, ("z", "c"), halves)
    up3c, down3c = lax.ppermute(up3, "c", swap), lax.ppermute(down3, "c", swap)
    near = [pair, up1, down1, up2, down2, up3, down3]
    near += [pair_c, up1c, down1c, up2c, down2c, up3c, down3c]
    acc, lse = pl.pallas_call(
        near_kernel,
        out_shape=(jax.ShapeDtypeStruct((2, 1024, HD), F32),) * 2,
        in_specs=[hbm] * (2 * NEAR) + [spec()],
        out_specs=[spec()] * 2,
        scratch_shapes=scratch(NEAR),
        compiler_params=pltpu.CompilerParams(vmem_limit_bytes=24 << 20),
        cost_estimate=cost(NEAR),
        name="self_near",
    )(*near, self_q[0])

    last, acc = tie((last, acc))
    last_c = lax.ppermute(last, "c", swap)
    mixed = pl.pallas_call(
        far_kernel,
        out_shape=jax.ShapeDtypeStruct((128, 16, HD), BF16),
        in_specs=[hbm] * (2 * FAR) + [spec()] * 4,
        out_specs=spec(),
        scratch_shapes=scratch(FAR),
        compiler_params=pltpu.CompilerParams(vmem_limit_bytes=24 << 20),
        cost_estimate=cost(FAR),
        name="self_far",
    )(last, last_c, self_q[0], acc, lse, cross)

    pieces, mixed = tie((pieces, mixed))
    image_grads = pl.pallas_call(
        sum_kernel,
        out_shape=jax.ShapeDtypeStruct((8, 2, 2 * HD), F32),
        in_specs=[spec()],
        out_specs=spec(),
        name="sum_pieces",
    )(pieces)
    return (mixed[None], grad_q[None], image_grads)


def solution(mesh):
    fine = Mesh(mesh.devices.reshape(4, 8, 2, 2, 2), ("y", "z", "x", "c", "t"))
    rows = P("y", ("z", "x", "c"), "t", None)
    image = P(("y", "z", "x", "c"), "t", None)
    return jax.shard_map(
        shards,
        mesh=fine,
        in_specs=(rows, rows, rows, image, P("y", "t"), P(("z", "x", "c"), None), P(), rows),
        out_specs=(rows, rows, image),
        check_vma=False,
    )
```

```python
import math

import jax
import jax.numpy as jnp
from jax import lax
from jax.experimental import pallas as pl
from jax.experimental.pallas import tpu as pltpu
from jax.sharding import Mesh, PartitionSpec as P

IMAGES = 4
BLOCK = 64
HD = 128
NEG = -1e30
F32 = jnp.float32
BF16 = jnp.bfloat16
SCALE = 1.0 / math.sqrt(HD)
SCALE2 = SCALE / math.log(2.0)
NT = (((1,), (1,)), ((), ()))


def nt(a, b):
    return lax.dot_general(a, b, NT, preferred_element_type=F32)


def nn(a, b):
    return jnp.dot(a, b, preferred_element_type=F32)


def flip(a):
    return jnp.transpose(a.astype(F32), (1, 0)).astype(a.dtype)


def info_kernel(image_ref, mask_ref, gate_ref, bias_ref, gate_out):
    core = lax.axis_index("c")
    count = bias_ref.shape[1]
    half = count // 2
    lane = lax.broadcasted_iota(jnp.int32, (1, count), 1)
    which = jnp.where(lane < half, core, 1 - core)
    part = lane % half // 8
    token = (((part // 16 * 8 + part % 8) * 2 + part // 8 % 2) * 2 + which) * 8 + lane % 8
    for rb in range(2):
        on = jnp.zeros((1, count), jnp.int32) + mask_ref[rb, 0]
        bound = 0
        for k in range(IMAGES - 1):
            bound = bound + image_ref[k]
            on = jnp.where(token >= bound, mask_ref[rb, k + 1], on)
        bias_ref[rb : rb + 1, :] = jnp.where(on == 1, 0.0, NEG)
    head = lax.broadcasted_iota(jnp.int32, (16, 16), 0)
    chosen = lax.broadcasted_iota(jnp.int32, (16, 16), 1) == head
    gates = jnp.where(chosen, jnp.broadcast_to(gate_ref[...], (16, 16)), 0.0)
    gate_out[...] = jnp.tanh(jnp.broadcast_to(jnp.sum(gates, axis=1, keepdims=True), (16, HD)))


def cross_kernel(
    bias_ref, cq_ref, cot_ref, gate_ref, va_ref, vb_ref, out_ref, gq_ref, ga_ref, gb_ref
):
    half = va_ref.shape[0]
    count = 2 * half
    rows = cq_ref.shape[0] * 8
    bias = jnp.concatenate(
        [jnp.broadcast_to(bias_ref[rb : rb + 1, :], (rows // 2, count)) for rb in range(2)], axis=0
    )
    gate = gate_ref[...]
    keys = jnp.concatenate([va_ref[:, :HD], vb_ref[:, :HD]], axis=0)
    values = jnp.concatenate([va_ref[:, HD:], vb_ref[:, HD:]], axis=0)
    q = cq_ref[...].reshape(rows, HD)
    go = (cot_ref[...].astype(F32) * gate[None]).astype(BF16).reshape(rows, HD)
    s = nt(q, keys) * SCALE2 + bias
    top = jnp.max(s, axis=1, keepdims=True)
    top = jnp.where(top < 0.5 * NEG, 0.0, top)
    p = jnp.exp2(s - top)
    pb = p.astype(BF16)
    both = nn(pb, with_ones(values))
    inv = 1.0 / jnp.maximum(both[:, HD:], 1.0)
    cross = both[:, :HD] * inv
    out_ref[...] = cross.reshape(rows // 8, 8, HD) * gate[None]
    dot = jnp.sum(go.astype(F32) * cross, axis=1, keepdims=True)
    ds = (p * (nt(go, values) - dot)).astype(BF16)
    gq_ref[...] = (nn(ds, keys) * (inv * SCALE)).reshape(rows // 8, 8, HD).astype(BF16)
    qs = (q.astype(F32) * (inv * SCALE)).astype(BF16)
    gs = (go.astype(F32) * inv).astype(BF16)
    dk = jnp.transpose(nn(flip(qs), ds), (1, 0))
    dv = jnp.transpose(nn(flip(gs), pb), (1, 0))
    ga_ref[:, :HD] = dk[:half]
    ga_ref[:, HD:] = dv[:half]
    gb_ref[:, :HD] = dk[half:].astype(BF16)
    gb_ref[:, HD:] = dv[half:].astype(BF16)


LOCAL = 512
TILE = 256


def attend(q, keys, values, limit, top, total, acc):
    s = nt(q, keys) * SCALE2
    if limit is not None:
        s = jnp.where(limit, s, NEG)
    new = jnp.maximum(top, jnp.broadcast_to(jnp.max(s, axis=1, keepdims=True), top.shape))
    factor = jnp.exp2(top - new)
    p = jnp.exp2(s - jnp.tile(new, (1, keys.shape[0] // HD))).astype(BF16)
    both = nn(p, values)
    return new, total * factor + both[:, HD:], acc * factor + both[:, :HD]


def with_ones(values):
    return jnp.concatenate([values, jnp.ones_like(values)], axis=1)


def fetch_blocks(own_refs, other_refs, kv_ref, sems):
    half = LOCAL // 2
    for i, pair in enumerate(zip(own_refs, other_refs)):
        for side, source in enumerate(pair):
            target = kv_ref.at[i, pl.ds(side * half, half), :]
            pltpu.make_async_copy(source, target, sems.at[i, side]).start()


def wait_block(kv_ref, sems, block):
    half = LOCAL // 2
    for side in range(2):
        place = kv_ref.at[block, pl.ds(side * half, half), :]
        pltpu.make_async_copy(place, place, sems.at[block, side]).wait()


def blend(q_own, kv_ref, block, top_ref, sum_ref, acc_ref):
    for h in range(2):
        lane = h * 2 * HD
        keys = kv_ref[block, :, lane : lane + HD].reshape(-1, HD)
        values = with_ones(kv_ref[block, :, lane + HD : lane + 2 * HD].reshape(-1, HD))
        for t in range(1024 // TILE):
            cols = slice(t * TILE, (t + 1) * TILE)
            state = top_ref[h, cols, :], sum_ref[h, cols, :], acc_ref[h, cols, :]
            state = attend(q_own[h, cols, :], keys, values, None, *state)
            top_ref[h, cols, :], sum_ref[h, cols, :], acc_ref[h, cols, :] = state


NEAR = 7
FAR = 1


def near_kernel(*refs):
    own_refs, other_refs = refs[:NEAR], refs[NEAR : 2 * NEAR]
    q_ref, acc_out, lse_out, kv_ref, acc_ref, top_ref, sum_ref, q_own, sems = refs[2 * NEAR :]
    fetch_blocks(own_refs, other_refs, kv_ref, sems)
    for h in range(2):
        q_own[h] = q_ref[:, h * 8 : h * 8 + 8, :].reshape(1024, HD)
    z = lax.axis_index("z")
    core = lax.axis_index("c")
    half = LOCAL // 2
    key = lax.broadcasted_iota(jnp.int32, (TILE, LOCAL), 1)
    from_core = jnp.where(key < half, core, 1 - core)
    place = key % half
    place = (place // 128) * 256 + from_core * 128 + place % 128
    row = lax.broadcasted_iota(jnp.int32, (TILE, LOCAL), 0) // 8
    row = row + lax.axis_index("x") * 256 + core * 128
    start = jnp.full((TILE, HD), NEG, F32)
    zero = jnp.zeros((TILE, HD), F32)
    wait_block(kv_ref, sems, 0)
    for h in range(2):
        lane = h * 2 * HD
        keys = kv_ref[0, :, lane : lane + HD]
        values = with_ones(kv_ref[0, :, lane + HD : lane + 2 * HD])
        for t in range(1024 // TILE):
            cols = slice(t * TILE, (t + 1) * TILE)
            limit = place <= row + t * (TILE // 8)
            state = attend(q_own[h, cols, :], keys, values, limit, start, zero, zero)
            top_ref[h, cols, :], sum_ref[h, cols, :], acc_ref[h, cols, :] = state

    @pl.loop(1, NEAR // 2 + 1)
    def _(step):
        first = 2 * step - 1
        wait_block(kv_ref, sems, first)
        wait_block(kv_ref, sems, first + 1)
        up = z >= step
        down = z + step >= 8

        @pl.when(jnp.logical_and(up, down))
        def _():
            blend(q_own, kv_ref, pl.ds(first, 2), top_ref, sum_ref, acc_ref)

        @pl.when(jnp.logical_xor(up, down))
        def _():
            blend(q_own, kv_ref, jnp.where(up, first, first + 1), top_ref, sum_ref, acc_ref)

    acc_out[...] = acc_ref[...] / sum_ref[...]
    lse_out[...] = top_ref[...] + jnp.log2(sum_ref[...])


def far_kernel(*refs):
    own_ref, other_ref, q_ref, acc_in, lse_in, cross_ref, out_ref = refs[:7]
    kv_ref, acc_ref, top_ref, sum_ref, q_own, sems = refs[7:]
    fetch_blocks([own_ref], [other_ref], kv_ref, sems)
    for h in range(2):
        q_own[h] = q_ref[:, h * 8 : h * 8 + 8, :].reshape(1024, HD)
    acc_ref[...] = acc_in[...]
    top_ref[...] = lse_in[...]
    sum_ref[...] = jnp.ones_like(sum_ref)
    wait_block(kv_ref, sems, 0)

    @pl.when(lax.axis_index("z") >= 4)
    def _():
        blend(q_own, kv_ref, 0, top_ref, sum_ref, acc_ref)

    for h in range(2):
        mixed = (acc_ref[h] / sum_ref[h]).reshape(2 * BLOCK, 8, HD)
        out_ref[:, h * 8 : h * 8 + 8, :] = (mixed + cross_ref[:, h * 8 : h * 8 + 8, :]).astype(BF16)


def sum_kernel(pieces_ref, out_ref):
    total = jnp.sum(pieces_ref[...].astype(F32), axis=0)
    for h in range(2):
        out_ref[:, h, :] = total[:, h * 2 * HD : (h + 1) * 2 * HD]


def pair_kernel(own_ref, other_ref, out_ref):
    x = lax.axis_index("x")
    rows = own_ref.shape[0]
    out_ref[pl.ds(pl.multiple_of(x * rows, rows), rows), :] = own_ref[...]
    out_ref[pl.ds(pl.multiple_of((1 - x) * rows, rows), rows), :] = other_ref[...]


def pick_kernel(first_ref, second_ref, out_ref):
    core = lax.axis_index("c")

    @pl.when(core == 0)
    def _():
        out_ref[...] = first_ref[...]

    @pl.when(core == 1)
    def _():
        out_ref[...] = second_ref[...]


def spec():
    return pl.BlockSpec(memory_space=pltpu.VMEM)


def shards(
    self_q, self_kv, cross_q, vision_kv, cross_gate, cross_mask, image_tokens, out_cotangent
):
    swap = [(0, 1), (1, 0)]
    up = [(i, (i + 1) % 8) for i in range(8)]
    down = [(i, (i + 7) % 8) for i in range(8)]
    ring = ("y", "x", "z")
    parts = lax.axis_size(ring)
    tokens = parts * 8
    tie = lax.optimization_barrier

    image = jnp.broadcast_to(vision_kv.reshape(1, 8, 4 * HD), (8, 8, 4 * HD))
    kv = self_kv.reshape(128, 4 * HD)
    other = lax.ppermute(kv, "x", swap)
    column = lax.all_to_all(image, "z", 0, 0, tiled=True).reshape(1, 64, 4 * HD)
    column, kv, other = tie((column, kv, other))
    pair = pl.pallas_call(
        pair_kernel,
        out_shape=jax.ShapeDtypeStruct((256, 4 * HD), BF16),
        in_specs=[spec()] * 2,
        out_specs=spec(),
        compiler_params=pltpu.CompilerParams(vmem_limit_bytes=4 << 20),
        name="pair",
    )(kv, other)
    va = lax.all_to_all(
        jnp.broadcast_to(column, (8, 64, 4 * HD)), ("y", "x"), 0, 0, tiled=True
    ).reshape(tokens, 4 * HD)
    up1, down1 = lax.ppermute(pair, "z", up), lax.ppermute(pair, "z", down)
    pair_c = lax.ppermute(pair, "c", swap)

    smem = pl.BlockSpec(memory_space=pltpu.SMEM)
    bias, gate = pl.pallas_call(
        info_kernel,
        out_shape=(
            jax.ShapeDtypeStruct((2, 2 * tokens), F32),
            jax.ShapeDtypeStruct((16, HD), F32),
        ),
        in_specs=[smem, smem, spec()],
        out_specs=[spec()] * 2,
        compiler_params=pltpu.CompilerParams(vmem_limit_bytes=4 << 20),
        name="mask_and_gate",
    )(image_tokens, cross_mask, cross_gate)
    va, up1, down1, pair_c, bias, gate = tie((va, up1, down1, pair_c, bias, gate))
    vb = lax.ppermute(va, "c", swap)
    up2, down2 = lax.ppermute(up1, "z", up), lax.ppermute(down1, "z", down)
    up1c, down1c = lax.ppermute(up1, "c", swap), lax.ppermute(down1, "c", swap)

    by_head = pl.BlockSpec((128, 8, HD), lambda h: (0, h, 0))
    by_lane = pl.BlockSpec((tokens, 2 * HD), lambda h: (0, h))
    cross, grad_q, grad_own, grad_other = pl.pallas_call(
        cross_kernel,
        grid=(2,),
        out_shape=(
            jax.ShapeDtypeStruct((128, 16, HD), F32),
            jax.ShapeDtypeStruct((128, 16, HD), BF16),
            jax.ShapeDtypeStruct((tokens, 4 * HD), F32),
            jax.ShapeDtypeStruct((tokens, 4 * HD), BF16),
        ),
        in_specs=[
            spec(),
            by_head,
            by_head,
            pl.BlockSpec((8, HD), lambda h: (h, 0)),
            by_lane,
            by_lane,
        ],
        out_specs=[by_head, by_head, by_lane, by_lane],
        compiler_params=pltpu.CompilerParams(vmem_limit_bytes=40 << 20),
        cost_estimate=pl.CostEstimate(
            flops=6 * 2 * 2 * 1024 * 1024 * 128, bytes_accessed=6 << 20, transcendentals=2 << 20
        ),
        name="cross_attention",
    )(bias, cross_q[0], out_cotangent[0], gate, va, vb)

    grad_other, up1c, down1c, up2, down2 = tie((grad_other, up1c, down1c, up2, down2))
    received = lax.ppermute(grad_other, "c", swap)
    up3, down3 = lax.ppermute(up2, "z", up), lax.ppermute(down2, "z", down)
    up2c, down2c = lax.ppermute(up2, "c", swap), lax.ppermute(down2, "c", swap)
    partial = (grad_own + received.astype(F32)).astype(BF16).reshape(parts, 8, 4 * HD)
    partial, up2c, down2c = tie((partial, up2c, down2c))
    pieces = lax.all_to_all(partial, ring, 0, 0, tiled=True)

    hbm = pl.BlockSpec(memory_space=pl.ANY)

    def scratch(count):
        return [
            pltpu.VMEM((count, LOCAL, 4 * HD), BF16),
            pltpu.VMEM((2, 1024, HD), F32),
            pltpu.VMEM((2, 1024, HD), F32),
            pltpu.VMEM((2, 1024, HD), F32),
            pltpu.VMEM((2, 1024, HD), BF16),
            pltpu.SemaphoreType.DMA((count, 2)),
        ]

    def cost(count):
        return pl.CostEstimate(
            flops=count * 2 * 2 * 2 * 512 * 1024 * 128,
            bytes_accessed=6 << 20,
            transcendentals=count << 20,
        )

    split = pl.pallas_call(
        pick_kernel,
        out_shape=jax.ShapeDtypeStruct(up3.shape, BF16),
        in_specs=[spec()] * 2,
        out_specs=spec(),
        compiler_params=pltpu.CompilerParams(vmem_limit_bytes=4 << 20),
        name="pick",
    )(up3, down3)
    halves = [
        ((zi + (1 if ci else 7)) % 8 * 2 + ci, zi * 2 + ci) for zi in range(4, 8) for ci in range(2)
    ]
    last = lax.ppermute(split, ("z", "c"), halves)
    up3c, down3c = lax.ppermute(up3, "c", swap), lax.ppermute(down3, "c", swap)
    near = [pair, up1, down1, up2, down2, up3, down3]
    near += [pair_c, up1c, down1c, up2c, down2c, up3c, down3c]
    acc, lse = pl.pallas_call(
        near_kernel,
        out_shape=(jax.ShapeDtypeStruct((2, 1024, HD), F32),) * 2,
        in_specs=[hbm] * (2 * NEAR) + [spec()],
        out_specs=[spec()] * 2,
        scratch_shapes=scratch(NEAR),
        compiler_params=pltpu.CompilerParams(vmem_limit_bytes=24 << 20),
        cost_estimate=cost(NEAR),
        name="self_near",
    )(*near, self_q[0])

    last, acc = tie((last, acc))
    last_c = lax.ppermute(last, "c", swap)
    mixed = pl.pallas_call(
        far_kernel,
        out_shape=jax.ShapeDtypeStruct((128, 16, HD), BF16),
        in_specs=[hbm] * (2 * FAR) + [spec()] * 4,
        out_specs=spec(),
        scratch_shapes=scratch(FAR),
        compiler_params=pltpu.CompilerParams(vmem_limit_bytes=24 << 20),
        cost_estimate=cost(FAR),
        name="self_far",
    )(last, last_c, self_q[0], acc, lse, cross)

    pieces, mixed = tie((pieces, mixed))
    image_grads = pl.pallas_call(
        sum_kernel,
        out_shape=jax.ShapeDtypeStruct((8, 2, 2 * HD), F32),
        in_specs=[spec()],
        out_specs=spec(),
        name="sum_pieces",
    )(pieces)
    return (mixed[None], grad_q[None], image_grads)


def solution(mesh):
    fine = Mesh(mesh.devices.reshape(4, 8, 2, 2, 2), ("y", "z", "x", "c", "t"))
    rows = P("y", ("z", "x", "c"), "t", None)
    image = P(("y", "z", "x", "c"), "t", None)
    return jax.shard_map(
        shards,
        mesh=fine,
        in_specs=(rows, rows, rows, image, P("y", "t"), P(("z", "x", "c"), None), P(), rows),
        out_specs=(rows, rows, image),
        check_vma=False,
    )
```
